256 devices in a mesh: ctx: 16 (over x, y), own: 16 (over z, core).
Axes of the slice: x: 4, y: 4, z: 8, core: 2. Of those that a mesh axis runs over, the one named last changes fastest.
Arguments:
- queries: bfloat16 [16, 8192, 1024], P('own', 'ctx'), may hold values from -6 to 6
- key_states: bfloat16 [16, 8192, 1024], P('own', 'ctx'), may hold values from -6 to 6
- value_states: bfloat16 [16, 8192, 1024], P('own', 'ctx'), may hold values from -6 to 6
- grad_output: bfloat16 [16, 8192, 1024], P('own', 'ctx'), may hold values from -6 to 6
- block_lists: int32 [16, 64, 8], P('ctx'), may hold values from 0 to 63, as said below
- dest_rows: int32 [16, 8192], P('own', 'ctx'), may hold values from 0 to 131071, as said below
Outputs:
- pool_grad: bfloat16 [16, 8192, 3072], P('own', 'ctx')
The draws below stay inside these ranges and needn't reach their ends.
Inputs may be any that keep to these rules, and one draw needn't show every extreme that they name: `block_lists`: each list names 8 distinct blocks, among them the query block itself. `dest_rows`: each pool row is named exactly once; a position's pool row lies in the same block of 512 positions; of the 512 positions of one device at most 128 have pool rows in one sequence, and exactly 128 do for some sequence on every device.
All inputs are finite; a program needn't handle non-finite values.
Results may differ from the reference program's by a relative error of at most 0.0071.
Values may be sent and summed in bfloat16 or wider, within the bound.
No kernel may reach another device: no remote copies, remote signals or barrier semaphores. Data moves between devices by JAX's collectives and lax.ppermute only.
A program may use at most 128 MiB of HBM per device.

```python
import jax
import jax.numpy as jnp
from jax import lax

H = 16
HD = 64
D = 1024
BLK = 128
KB = 8
TOK_DEV = 512
LENGTH = 8192
SEQS = 16


def draw_queries(key, part):
    key = jax.random.fold_in(key, 1)
    shape = (SEQS, LENGTH, H * HD)
    return jnp.clip(jax.random.normal(key, shape, jnp.float32), -5.0, 5.0).astype(jnp.bfloat16)


def draw_key_states(key, part):
    key = jax.random.fold_in(key, 2)
    shape = (SEQS, LENGTH, H * HD)
    return jnp.clip(jax.random.normal(key, shape, jnp.float32), -5.0, 5.0).astype(jnp.bfloat16)


def draw_block_lists(key, part):
    key = jax.random.fold_in(key, 3)
    block_count = LENGTH // BLK

    def one_list(head_index, block_index):
        sub_key = jax.random.fold_in(jax.random.fold_in(key, head_index), block_index)
        others = jax.random.permutation(sub_key, block_count - 1)[:KB - 1]
        chosen = (block_index + 1 + others) % block_count
        return jnp.concatenate([jnp.reshape(block_index, (1,)), chosen]).astype(jnp.int32)
    heads_grid = jnp.repeat(jnp.arange(H, dtype=jnp.int32), block_count)
    blocks_grid = jnp.tile(jnp.arange(block_count, dtype=jnp.int32), H)
    lists = jax.vmap(one_list)(heads_grid, blocks_grid)
    return lists.reshape(H, block_count, KB)


def draw_dest_rows(key, part):
    key = jax.random.fold_in(key, 5)
    shares = jnp.array([2, 2, 1, 1, 1, 1], jnp.int32) * (TOK_DEV // 8)
    ends = jnp.cumsum(shares)
    rank_index = jnp.arange(TOK_DEV, dtype=jnp.int32)
    group_index = jnp.sum((rank_index[:, None] >= ends[None, :]).astype(jnp.int32), axis=1)
    seq_range = jnp.arange(SEQS, dtype=jnp.int32)

    def column(column_index):
        sub_key = jax.random.fold_in(key, column_index)
        shifts = jax.random.permutation(jax.random.fold_in(sub_key, 0), SEQS)[:6].astype(jnp.int32)
        source_perm = jax.vmap(lambda seq_index: jax.random.permutation(jax.random.fold_in(jax.random.fold_in(sub_key, 1), seq_index), TOK_DEV))(seq_range).astype(jnp.int32)
        target_perm = jax.vmap(lambda seq_index: jax.random.permutation(jax.random.fold_in(jax.random.fold_in(sub_key, 2), seq_index), TOK_DEV))(seq_range).astype(jnp.int32)
        owner_index = (seq_range[:, None] + shifts[group_index][None, :]) % SEQS
        local_row = target_perm[owner_index, rank_index[None, :]]
        targets = owner_index * LENGTH + column_index * TOK_DEV + local_row
        result = jnp.zeros((SEQS, TOK_DEV), jnp.int32)
        return result.at[seq_range[:, None], source_perm].set(targets)
    columns = jax.vmap(column)(jnp.arange(LENGTH // TOK_DEV, dtype=jnp.int32))
    return columns.transpose(1, 0, 2).reshape(SEQS, LENGTH).astype(jnp.int32)


def level_of(stream_key, extent, split, smallest, high):
    loudness, own = 1.0, jax.random.fold_in(stream_key, 6)
    for axis_at, parts in split:
        draws = jnp.exp(jax.random.uniform(jax.random.fold_in(own, axis_at), (parts,), jnp.float32, smallest / len(split), high / len(split)))
        loudness = loudness * jnp.repeat(draws, extent[axis_at] // parts).reshape([-1 if axis == axis_at else 1 for axis in range(len(extent))])
    return loudness


def gaussian(rng, dims, width, limit, split=(), held_as=jnp.bfloat16):
    entries = width * jax.random.normal(rng, dims, jnp.float32)
    if split:
        entries = entries * level_of(rng, dims, split, -0.22, 0.18)
    return jnp.clip(entries, -limit, limit).astype(held_as)


def setup_inputs(seed: int = 0) -> dict:
    key_list = jax.random.split(jax.random.key(seed), 7)
    queries = draw_queries(jax.random.fold_in(key_list[6], 71), 0)
    key_states = draw_key_states(jax.random.fold_in(key_list[6], 71), 0)
    value_states = gaussian(key_list[2], (SEQS, LENGTH, D), 1.0, 6.0, ((0, 16), (1, 16)))
    grad_output = gaussian(key_list[3], (SEQS, LENGTH, D), 1.0, 6.0, ((0, 16), (1, 16)))
    block_lists = draw_block_lists(jax.random.fold_in(key_list[6], 71), 0)
    dest_rows = draw_dest_rows(jax.random.fold_in(key_list[6], 71), 0)
    return dict(queries=queries, key_states=key_states, value_states=value_states, grad_output=grad_output, block_lists=block_lists, dest_rows=dest_rows)


def head_grads(query_rows, key_rows, value_rows, grad_rows, lists):
    block_count, list_width = lists.shape
    block_rows = query_rows.shape[0] // block_count
    head_dim = query_rows.shape[1]
    key_blocks = key_rows.reshape(block_count, block_rows, head_dim)
    value_blocks = value_rows.reshape(block_count, block_rows, head_dim)

    def step(running, index):
        key_total, value_total = running
        chosen = lists[index]
        query_block = lax.dynamic_slice_in_dim(query_rows, index * block_rows, block_rows, 0)
        grad_block = lax.dynamic_slice_in_dim(grad_rows, index * block_rows, block_rows, 0)
        key_chosen = key_blocks[chosen].reshape(list_width * block_rows, head_dim)
        value_chosen = value_blocks[chosen].reshape(list_width * block_rows, head_dim)
        scores = jnp.dot(query_block, key_chosen.T, preferred_element_type=jnp.float32) * 0.125
        row_max = jnp.max(scores, axis=1, keepdims=True)
        exp_scores = jnp.exp(scores - row_max)
        weights = exp_scores / jnp.sum(exp_scores, axis=1, keepdims=True)
        weights_half = weights.astype(jnp.bfloat16)
        grad_weights = jnp.dot(grad_block, value_chosen.T, preferred_element_type=jnp.float32)
        row_delta = jnp.sum(weights * grad_weights, axis=1, keepdims=True)
        grad_scores = (0.125 * weights * (grad_weights - row_delta)).astype(jnp.bfloat16)
        grad_query = jnp.dot(grad_scores, key_chosen, preferred_element_type=jnp.float32).astype(jnp.bfloat16)
        key_part = jnp.dot(grad_scores.T, query_block, preferred_element_type=jnp.float32)
        value_part = jnp.dot(weights_half.T, grad_block, preferred_element_type=jnp.float32)
        key_total = key_total.at[chosen].add(key_part.reshape(list_width, block_rows, head_dim))
        value_total = value_total.at[chosen].add(value_part.reshape(list_width, block_rows, head_dim))
        return (key_total, value_total), grad_query

    zeros = jnp.zeros((block_count, block_rows, head_dim), jnp.float32)
    (key_total, value_total), grad_query = lax.scan(step, (zeros, zeros), jnp.arange(block_count, dtype=jnp.int32))
    return (grad_query.reshape(-1, head_dim),
            key_total.reshape(-1, head_dim).astype(jnp.bfloat16),
            value_total.reshape(-1, head_dim).astype(jnp.bfloat16))


def reference(queries, key_states, value_states, grad_output, block_lists, dest_rows):
    seq_count, length, model_width = queries.shape
    head_dim = model_width // H

    def one_head(index):
        seq_index = index // H
        head_index = index % H

        def pick(array):
            seq_rows = lax.dynamic_index_in_dim(array, seq_index, 0, keepdims=False)
            return lax.dynamic_slice_in_dim(seq_rows, head_index * head_dim, head_dim, 1)

        lists = lax.dynamic_index_in_dim(block_lists, head_index, 0, keepdims=False)
        result = head_grads(pick(queries), pick(key_states), pick(value_states), pick(grad_output), lists)
        return jnp.stack(result, axis=1)

    per_head = lax.map(one_head, jnp.arange(seq_count * H, dtype=jnp.int32))
    per_head = per_head.reshape(seq_count, H, length, 3, head_dim).transpose(0, 2, 3, 1, 4)
    per_head = per_head.reshape(seq_count * length, 3 * model_width)
    pool = jnp.zeros_like(per_head).at[dest_rows.reshape(-1)].set(per_head)
    return pool.reshape(seq_count, length, 3 * model_width)
```

```python
import functools

import jax
import jax.numpy as jnp
from jax import lax
from jax.experimental import pallas as pl
from jax.experimental.pallas import tpu as pltpu
from jax.sharding import PartitionSpec as P

H = 16
HD = 64
BLK = 128
KB = 8
COLS = 16
TOK = 512
OWNERS = 16
LENGTH = 8192
BLOCKS = LENGTH // BLK
CLASSES = (640, 704, 768, 832, 896, 1024, 1280, 2048)
CAP_MAX = 2048
VMEM_LIMIT = 60 * 1024 * 1024
LOG2E = 1.4426950408889634

VMEM = pl.BlockSpec(memory_space=pltpu.VMEM)
SMEM = pl.BlockSpec(memory_space=pltpu.SMEM)
PARAMS = pltpu.CompilerParams(vmem_limit_bytes=VMEM_LIMIT)


def call(kernel, out_shape, in_specs, out_specs, scratch=(), flops=0, nbytes=1 << 20):
    return pl.pallas_call(
        kernel,
        out_shape=out_shape,
        in_specs=in_specs,
        out_specs=out_specs,
        scratch_shapes=list(scratch),
        compiler_params=PARAMS,
        cost_estimate=pl.CostEstimate(flops=flops, bytes_accessed=nbytes, transcendentals=0),
    )


def interleave_kernel(a_ref, b_ref, out_ref):
    for pair in range(H // 2):
        lanes = slice(pair * 128, pair * 128 + 128)
        a = a_ref[:, lanes]
        b = b_ref[:, lanes]
        out_ref[2 * pair] = jnp.concatenate([a[:, :HD], b[:, :HD]], axis=1)
        out_ref[2 * pair + 1] = jnp.concatenate([a[:, HD:], b[:, HD:]], axis=1)


def interleave(a, b):
    return call(
        interleave_kernel,
        jax.ShapeDtypeStruct((H, TOK, 2 * HD), jnp.bfloat16),
        [VMEM, VMEM],
        VMEM,
        nbytes=1 << 22,
    )(a, b)


def attention_kernel(lists_ref, qg_ref, kv_ref, dq_ref, dkv_ref, kt_ref):
    lane = lax.broadcasted_iota(jnp.int32, (BLK, 2 * HD), 1)

    def prepare(block, carry):
        rows = pl.ds(pl.multiple_of(block * BLK, BLK), BLK)
        kt_ref[:, rows] = kv_ref[rows, :].T[:HD]
        dkv_ref[rows, :] = jnp.zeros((BLK, 2 * HD), jnp.float32)
        return carry

    lax.fori_loop(0, BLOCKS, prepare, 0)

    def step(block, carry):
        rows = pl.ds(pl.multiple_of(block * BLK, BLK), BLK)
        qg = qg_ref[rows, :]
        zero = jnp.zeros_like(qg)
        diag = jnp.concatenate(
            [jnp.where(lane < HD, qg, zero), jnp.where(lane >= HD, qg, zero)], axis=0
        )
        places = [pl.multiple_of(lists_ref[block * KB + j] * BLK, BLK) for j in range(KB)]
        both = [
            lax.dot_general(
                kv_ref[pl.ds(places[j], BLK), :],
                diag,
                (((1,), (1,)), ((), ())),
                preferred_element_type=jnp.float32,
            )
            for j in range(KB)
        ]
        scores = [x[:, :BLK] for x in both]
        grads = [x[:, BLK:] for x in both]
        top = scores[0]
        for j in range(1, KB):
            top = jnp.maximum(top, scores[j])
        row_max = jnp.max(top, axis=0, keepdims=True)
        exps = [jnp.exp2((s - row_max) * (0.125 * LOG2E)) for s in scores]
        total = exps[0]
        mixed = exps[0] * grads[0]
        for j in range(1, KB):
            total = total + exps[j]
            mixed = mixed + exps[j] * grads[j]
        inverse = 1.0 / jnp.sum(total, axis=0, keepdims=True)
        delta = jnp.sum(mixed, axis=0, keepdims=True) * inverse
        dq = jnp.zeros((HD, BLK), jnp.float32)
        for j in range(KB):
            weights = exps[j] * inverse
            ds = (weights * (grads[j] - delta)).astype(jnp.bfloat16)
            pair = jnp.concatenate([ds, weights.astype(jnp.bfloat16)], axis=1)
            part = lax.dot_general(
                pair, diag, (((1,), (0,)), ((), ())), preferred_element_type=jnp.float32
            )
            at = pl.ds(places[j], BLK)
            dkv_ref[at, :] = dkv_ref[at, :] + part
            dq = dq + lax.dot_general(
                kt_ref[:, at], ds, (((1,), (0,)), ((), ())), preferred_element_type=jnp.float32
            )
        dq = jnp.concatenate([dq * 0.125, jnp.zeros((HD, BLK), jnp.float32)], axis=0)
        dq_ref[rows, :] = dq.T
        return carry

    lax.fori_loop(0, BLOCKS, step, 0)

    def finish(block, carry):
        rows = pl.ds(pl.multiple_of(block * BLK, BLK), BLK)
        x = dkv_ref[rows, :]
        dkv_ref[rows, :] = jnp.where(lane < HD, x * 0.125, x)
        return carry

    lax.fori_loop(0, BLOCKS, finish, 0)


def attention(lists, qg, kv):
    out = jax.ShapeDtypeStruct((LENGTH, 2 * HD), jnp.float32)
    return call(
        attention_kernel,
        (out, out),
        [SMEM, VMEM, VMEM],
        (VMEM, VMEM),
        [pltpu.VMEM((HD, LENGTH), jnp.bfloat16)],
        flops=6 * BLOCKS * KB * BLK * BLK * HD * 2 * 8,
        nbytes=12 << 20,
    )(lists, qg, kv)


def place_kernel(slots_ref, pool_rows_ref, counts_ref, rows_ref):
    for owner in range(OWNERS):
        first = owner * CAP_MAX + counts_ref[owner]
        for k in range(8):

            @pl.when(counts_ref[owner] + k < CAP_MAX)
            def _():
                rows_ref[first + k] = LENGTH

    def body(i, carry):
        for k in range(16):
            at = i * 16 + k
            rows_ref[slots_ref[at]] = pool_rows_ref[at]
        return carry

    lax.fori_loop(0, LENGTH // 16, body, 0)


def place(slots, pool_rows, counts):
    return call(
        place_kernel,
        jax.ShapeDtypeStruct((OWNERS * CAP_MAX,), jnp.int32),
        [SMEM, SMEM, SMEM],
        SMEM,
        nbytes=16 << 20,
    )(slots, pool_rows, counts)


def pack_kernel(cap, split, slots_ref, table_ref, out_ref, held):
    def body(i, carry):
        for k in range(16):
            at = i * 16 + k
            held[pl.ds(slots_ref[at], 1), :] = table_ref[pl.ds(at, 1), :]
        return carry

    lax.fori_loop(0, LENGTH // 16, body, 0)
    half = cap // 2
    for owner in range(OWNERS):
        if split:
            left = held[owner * cap : owner * cap + half, :HD]
            right = held[owner * cap + half : (owner + 1) * cap, :HD]
            out_ref[owner] = jnp.concatenate([left, right], axis=1).astype(jnp.bfloat16)
        else:
            out_ref[owner] = held[owner * cap : (owner + 1) * cap, :].astype(jnp.bfloat16)


def pack(cap, split, slots, table):
    return call(
        functools.partial(pack_kernel, cap, split),
        jax.ShapeDtypeStruct((OWNERS, cap // 2 if split else cap, 2 * HD), jnp.bfloat16),
        [SMEM, VMEM],
        VMEM,
        [pltpu.VMEM((OWNERS * cap, 2 * HD), jnp.float32)],
        nbytes=16 << 20,
    )(slots, table)


def unpack_kernel(cap, split, rows_ref, counts_ref, in_ref, out_ref, held, placed):
    half = cap // 2
    for source in range(OWNERS):
        if split:
            x = in_ref[source].astype(jnp.float32)
            held[source * cap : source * cap + half, :HD] = x[:, :HD]
            held[source * cap + half : (source + 1) * cap, :HD] = x[:, HD:]
        else:
            held[source * cap : (source + 1) * cap, :] = in_ref[source].astype(jnp.float32)
    for source in range(OWNERS):

        def body(i, carry, source=source):
            for k in range(8):
                at = i * 8 + k
                placed[pl.ds(rows_ref[source * CAP_MAX + at], 1), :] = held[
                    pl.ds(source * cap + at, 1), :
                ]
            return carry

        lax.fori_loop(0, (counts_ref[source] + 7) // 8, body, 0)
    for column in range(COLS):
        if split:
            left = placed[column * TOK : column * TOK + TOK // 2, :HD]
            right = placed[column * TOK + TOK // 2 : (column + 1) * TOK, :HD]
            out_ref[column] = jnp.concatenate([left, right], axis=1).astype(jnp.bfloat16)
        else:
            out_ref[column] = placed[column * TOK : (column + 1) * TOK, :].astype(jnp.bfloat16)


def unpack(cap, split, rows, counts, buckets):
    return call(
        functools.partial(unpack_kernel, cap, split),
        jax.ShapeDtypeStruct((COLS, TOK // 2 if split else TOK, 2 * HD), jnp.bfloat16),
        [SMEM, SMEM, VMEM],
        VMEM,
        [
            pltpu.VMEM((OWNERS * cap, 2 * HD), jnp.float32),
            pltpu.VMEM((LENGTH + 8, 2 * HD), jnp.float32),
        ],
        nbytes=16 << 20,
    )(rows, counts, buckets)


def finish_kernel(dq_ref, dkv_ref, out_ref):
    half = TOK // 2
    width = H * HD
    for pair in range(H // 2):
        lanes = slice(pair * 128, pair * 128 + 128)
        first, second = dq_ref[2 * pair], dq_ref[2 * pair + 1]
        out_ref[:half, lanes] = jnp.concatenate([first[:, :HD], second[:, :HD]], axis=1)
        out_ref[half:, lanes] = jnp.concatenate([first[:, HD:], second[:, HD:]], axis=1)
        first, second = dkv_ref[2 * pair], dkv_ref[2 * pair + 1]
        at = width + pair * 128
        out_ref[:, at : at + 128] = jnp.concatenate([first[:, :HD], second[:, :HD]], axis=1)
        at = 2 * width + pair * 128
        out_ref[:, at : at + 128] = jnp.concatenate([first[:, HD:], second[:, HD:]], axis=1)


def finish(dq, dkv):
    return call(
        finish_kernel,
        jax.ShapeDtypeStruct((TOK, 3 * H * HD), jnp.bfloat16),
        [VMEM, VMEM],
        VMEM,
        nbytes=6 << 20,
    )(dq, dkv)


def swap(x, axis):
    return lax.all_to_all(x, axis, split_axis=0, concat_axis=0, tiled=True)


def ranks(owner):
    chosen = (
        owner.reshape(1, BLOCKS, BLK) == jnp.arange(OWNERS, dtype=jnp.int32)[:, None, None]
    ).astype(jnp.bfloat16)
    upto = jnp.triu(jnp.ones((BLK, BLK), jnp.bfloat16))
    inside = jnp.einsum("obi,ij->obj", chosen, upto, preferred_element_type=jnp.float32)
    totals = inside[:, :, -1]
    before = jnp.einsum(
        "ob,bc->oc",
        totals.astype(jnp.bfloat16),
        jnp.triu(jnp.ones((BLOCKS, BLOCKS), jnp.bfloat16), 1),
        preferred_element_type=jnp.float32,
    )
    rank = jnp.sum(chosen.astype(jnp.float32) * (inside + before[:, :, None]), axis=0) - 1.0
    counts = jnp.sum(totals, axis=1)
    return rank.reshape(-1).astype(jnp.int32), counts.astype(jnp.int32)


def per_device(queries, key_states, value_states, grad_output, block_lists, dest_rows):
    kv = swap(interleave(key_states[0], value_states[0]), "ctx").reshape(LENGTH, 2 * HD)
    qg = swap(interleave(queries[0], grad_output[0]), "ctx").reshape(LENGTH, 2 * HD)

    dest = lax.all_gather(dest_rows[0], "ctx", tiled=True)
    owner = dest // LENGTH
    rank, counts = ranks(owner)
    all_counts = lax.all_gather(counts, "own", tiled=False)
    largest = jnp.max(all_counts)
    incoming = lax.dynamic_index_in_dim(all_counts, lax.axis_index("own"), 1, keepdims=False)
    rows = place(owner * CAP_MAX + rank, dest - owner * LENGTH, counts)
    rows = swap(rows.reshape(OWNERS, CAP_MAX), "own").reshape(-1)

    dq, dkv = attention(block_lists[0].reshape(-1), qg, kv)

    def route(cap):
        def branch(owner, rank, rows, incoming, dq, dkv):
            slots = owner * cap + rank
            dkv_sent = swap(pack(cap, False, slots, dkv), "own")
            dq_sent = swap(pack(cap, True, slots, dq), "own")
            dkv_home = swap(unpack(cap, False, rows, incoming, dkv_sent), "ctx")
            dq_home = swap(unpack(cap, True, rows, incoming, dq_sent), "ctx")
            return dq_home, dkv_home

        return branch

    which = jnp.sum((largest > jnp.array(CLASSES[:-1], jnp.int32)).astype(jnp.int32))
    dq_home, dkv_home = lax.switch(
        which, [route(cap) for cap in CLASSES], owner, rank, rows, incoming, dq, dkv
    )
    return finish(dq_home, dkv_home)[None]


def solution(mesh):
    in_specs = (
        P("own", "ctx", None),
        P("own", "ctx", None),
        P("own", "ctx", None),
        P("own", "ctx", None),
        P("ctx", None, None),
        P("own", "ctx"),
    )
    out_specs = P("own", "ctx", None)
    return jax.shard_map(
        per_device, mesh=mesh, in_specs=in_specs, out_specs=out_specs, check_vma=False
    )
```

```python
import functools

import jax
import jax.numpy as jnp
from jax import lax
from jax.experimental import pallas as pl
from jax.experimental.pallas import tpu as pltpu
from jax.sharding import PartitionSpec as P

H = 16
HD = 64
BLK = 128
KB = 8
COLS = 16
TOK = 512
OWNERS = 16
LENGTH = 8192
BLOCKS = LENGTH // BLK
CLASSES = (640, 704, 768, 832, 896, 960, 1024, 1280, 2048)
CAP_MAX = 2048
STRIDE = CAP_MAX + 128
CODED = TOK + 16
EARLY = 12
VMEM_LIMIT = 60 * 1024 * 1024
LOG2E = 1.4426950408889634

VMEM = pl.BlockSpec(memory_space=pltpu.VMEM)
SMEM = pl.BlockSpec(memory_space=pltpu.SMEM)
PARAMS = pltpu.CompilerParams(vmem_limit_bytes=VMEM_LIMIT)


def call(kernel, out_shape, in_specs, out_specs, scratch=(), flops=0, nbytes=1 << 20):
    return pl.pallas_call(
        kernel,
        out_shape=out_shape,
        in_specs=in_specs,
        out_specs=out_specs,
        scratch_shapes=list(scratch),
        compiler_params=PARAMS,
        cost_estimate=pl.CostEstimate(flops=flops, bytes_accessed=nbytes, transcendentals=0),
    )


def interleave_kernel(a_ref, b_ref, out_ref):
    for pair in range(H // 2):
        lanes = slice(pair * 128, pair * 128 + 128)
        a = a_ref[:, lanes]
        b = b_ref[:, lanes]
        out_ref[2 * pair, :TOK] = jnp.concatenate([a[:, :HD], b[:, :HD]], axis=1)
        out_ref[2 * pair + 1, :TOK] = jnp.concatenate([a[:, HD:], b[:, HD:]], axis=1)


def interleave_with_dest_kernel(dest_ref, a_ref, b_ref, out_ref):
    interleave_kernel(a_ref, b_ref, out_ref)
    dest = dest_ref[...]
    coarse = (dest // LENGTH) * 4 + (dest % TOK) // 128
    codes = jnp.concatenate(
        [coarse, dest % 128, jnp.zeros((8, 128), jnp.int32)], axis=0
    ).astype(jnp.float32).astype(jnp.bfloat16)
    for head in range(H):
        out_ref[head, TOK:] = codes


def interleave(a, b):
    return call(
        interleave_kernel,
        jax.ShapeDtypeStruct((H, TOK, 2 * HD), jnp.bfloat16),
        [VMEM, VMEM],
        VMEM,
        nbytes=1 << 22,
    )(a, b)


def interleave_with_dest(dest, a, b):
    return call(
        interleave_with_dest_kernel,
        jax.ShapeDtypeStruct((H, CODED, 2 * HD), jnp.bfloat16),
        [VMEM, VMEM, VMEM],
        VMEM,
        nbytes=1 << 22,
    )(dest, a, b)


def coded_row(block):
    return pl.multiple_of((block // 4) * CODED + (block % 4) * BLK, 16)


def attention_kernel(lists_ref, qg_ref, kv_ref, dq_ref, dkv_ref, kt_ref):
    lane = lax.broadcasted_iota(jnp.int32, (BLK, 2 * HD), 1)
    depth = lax.broadcasted_iota(jnp.int32, (BLK, 2 * HD), 0)

    def prepare(block, carry):
        rows = pl.ds(pl.multiple_of(block * BLK, BLK), BLK)
        kt_ref[:, rows] = kv_ref[pl.ds(coded_row(block), BLK), :].T[:HD]
        dkv_ref[rows, :] = jnp.zeros((BLK, 2 * HD), jnp.float32)
        return carry

    lax.fori_loop(0, BLOCKS, prepare, 0)

    def step(block, carry):
        rows = pl.ds(pl.multiple_of(block * BLK, BLK), BLK)
        qg = qg_ref[rows, :]
        zero = jnp.zeros_like(qg)
        diag = jnp.concatenate(
            [jnp.where(lane < HD, qg, zero), jnp.where(lane >= HD, qg, zero)], axis=0
        )
        turned = qg.T
        first = jnp.where(depth < HD, turned, zero)
        second = jnp.where(depth >= HD, turned, zero)
        chosen = [lists_ref[block * KB + j] for j in range(KB)]
        places = [pl.multiple_of(c * BLK, BLK) for c in chosen]

        def product(c, right):
            return lax.dot_general(
                kv_ref[pl.ds(coded_row(c), BLK), :],
                right,
                (((1,), (0,)), ((), ())),
                preferred_element_type=jnp.float32,
            )

        scores = [product(c, first) for c in chosen]
        grads = [product(c, second) for c in chosen]
        top = scores[0]
        for j in range(1, KB):
            top = jnp.maximum(top, scores[j])
        row_max = jnp.max(top, axis=0, keepdims=True)
        exps = [jnp.exp2((s - row_max) * (0.125 * LOG2E)) for s in scores]
        total = exps[0]
        mixed = exps[0] * grads[0]
        for j in range(1, KB):
            total = total + exps[j]
            mixed = mixed + exps[j] * grads[j]
        inverse = 1.0 / jnp.sum(total, axis=0, keepdims=True)
        delta = jnp.sum(mixed, axis=0, keepdims=True) * inverse
        dq = jnp.zeros((HD, BLK), jnp.float32)
        for j in range(0, KB, 2):
            slopes, pairs = [], []
            for i in (j, j + 1):
                weights = exps[i] * inverse
                ds = (weights * (grads[i] - delta)).astype(jnp.bfloat16)
                slopes.append(ds)
                pairs.append(jnp.concatenate([ds, weights.astype(jnp.bfloat16)], axis=1))
            for i in (j, j + 1):
                part = lax.dot_general(
                    pairs[i - j], diag, (((1,), (0,)), ((), ())), preferred_element_type=jnp.float32
                )
                at = pl.ds(places[i], BLK)
                dkv_ref[at, :] = dkv_ref[at, :] + part
            dq = dq + lax.dot_general(
                jnp.concatenate([kt_ref[:, pl.ds(places[i], BLK)] for i in (j, j + 1)], axis=1),
                jnp.concatenate(slopes, axis=0),
                (((1,), (0,)), ((), ())), preferred_element_type=jnp.float32
            )
        dq = jnp.concatenate([dq * 0.125, jnp.zeros((HD, BLK), jnp.float32)], axis=0)
        dq_ref[rows, :] = dq.T
        return carry

    lax.fori_loop(0, BLOCKS, step, 0, unroll=8)

    def finish(block, carry):
        rows = pl.ds(pl.multiple_of(block * BLK, BLK), BLK)
        x = dkv_ref[rows, :]
        dkv_ref[rows, :] = jnp.where(lane < HD, x * 0.125, x)
        return carry

    lax.fori_loop(0, BLOCKS, finish, 0)


def attention(lists, qg, kv):
    out = jax.ShapeDtypeStruct((LENGTH, 2 * HD), jnp.float32)
    return call(
        attention_kernel,
        (out, out),
        [SMEM, VMEM, VMEM],
        (VMEM, VMEM),
        [pltpu.VMEM((HD, LENGTH), jnp.bfloat16)],
        flops=6 * BLOCKS * KB * BLK * BLK * HD * 2 * 8,
        nbytes=12 << 20,
    )(lists, qg, kv)


def place_kernel(slots_ref, pool_rows_ref, counts_ref, rows_ref):
    for owner in range(OWNERS):
        first = owner * STRIDE + counts_ref[owner]
        for k in range(8):
            rows_ref[first + k] = LENGTH

    def body(i, carry):
        for k in range(16):
            at = i * 16 + k
            rows_ref[slots_ref[at]] = pool_rows_ref[at]
        return carry

    lax.fori_loop(0, LENGTH // 16, body, 0)
    for owner in range(OWNERS):
        for k in range(OWNERS):
            rows_ref[owner * STRIDE + CAP_MAX + k] = counts_ref[k]


def place(slots, pool_rows, counts):
    return call(
        place_kernel,
        jax.ShapeDtypeStruct((OWNERS * STRIDE,), jnp.int32),
        [SMEM, SMEM, SMEM],
        SMEM,
        nbytes=16 << 20,
    )(slots, pool_rows, counts)


def pack_kernel(cap, split, slots_ref, table_ref, out_ref, held):
    def body(i, carry):
        for k in range(16):
            at = i * 16 + k
            held[pl.ds(slots_ref[at], 1), :] = table_ref[pl.ds(at, 1), :]
        return carry

    lax.fori_loop(0, LENGTH // 16, body, 0)
    half = cap // 2
    for owner in range(OWNERS):
        if split:
            left = held[owner * cap : owner * cap + half, :HD]
            right = held[owner * cap + half : (owner + 1) * cap, :HD]
            out_ref[owner] = jnp.concatenate([left, right], axis=1).astype(jnp.bfloat16)
        else:
            out_ref[owner] = held[owner * cap : (owner + 1) * cap, :].astype(jnp.bfloat16)


def pack(cap, split, slots, table):
    return call(
        functools.partial(pack_kernel, cap, split),
        jax.ShapeDtypeStruct((OWNERS, cap // 2 if split else cap, 2 * HD), jnp.bfloat16),
        [SMEM, VMEM],
        VMEM,
        [pltpu.VMEM((OWNERS * cap, 2 * HD), jnp.float32)],
        nbytes=16 << 20,
    )(slots, table)


def unpack_kernel(cap, split, me_ref, rows_ref, in_ref, *refs):
    *outs, held, placed = refs
    me_own, me_ctx = me_ref[0], me_ref[1]
    half = cap // 2
    for source in range(OWNERS):
        if split:
            x = in_ref[source].astype(jnp.float32)
            held[source * cap : source * cap + half, :HD] = x[:, :HD]
            held[source * cap + half : (source + 1) * cap, :HD] = x[:, HD:]
        else:
            held[source * cap : (source + 1) * cap, :] = in_ref[source].astype(jnp.float32)
    for source in range(OWNERS):
        count = rows_ref[source * STRIDE + CAP_MAX + me_own]

        def body(i, carry, source=source):
            for k in range(8):
                at = i * 8 + k
                placed[pl.ds(rows_ref[source * STRIDE + at], 1), :] = held[
                    pl.ds(source * cap + at, 1), :
                ]
            return carry

        lax.fori_loop(0, (count + 7) // 8, body, 0)
    if split:
        (out_ref,) = outs
        for column in range(COLS):
            left = placed[column * TOK : column * TOK + TOK // 2, :HD]
            right = placed[column * TOK + TOK // 2 : (column + 1) * TOK, :HD]
            out_ref[column] = jnp.concatenate([left, right], axis=1).astype(jnp.bfloat16)
    else:
        for d in range(COLS):
            first = pl.multiple_of((me_ctx ^ d) * TOK, TOK)
            outs[d][...] = placed[pl.ds(first, TOK), :].astype(jnp.bfloat16)


def unpack(cap, split, me, rows, buckets):
    piece = jax.ShapeDtypeStruct((TOK, 2 * HD), jnp.bfloat16)
    whole = jax.ShapeDtypeStruct((COLS, TOK // 2, 2 * HD), jnp.bfloat16)
    return call(
        functools.partial(unpack_kernel, cap, split),
        whole if split else [piece] * COLS,
        [SMEM, SMEM, VMEM],
        VMEM if split else [VMEM] * COLS,
        [
            pltpu.VMEM((OWNERS * cap, 2 * HD), jnp.float32),
            pltpu.VMEM((LENGTH + 8, 2 * HD), jnp.float32),
        ],
        nbytes=16 << 20,
    )(me, rows, buckets)


def finish_kernel(me_ref, dq_ref, *refs):
    *pieces, out_ref = refs
    me = me_ref[1]
    half = TOK // 2
    width = H * HD
    for pair in range(H // 2):
        lanes = slice(pair * 128, pair * 128 + 128)
        first, second = dq_ref[2 * pair], dq_ref[2 * pair + 1]
        out_ref[:half, lanes] = jnp.concatenate([first[:, :HD], second[:, :HD]], axis=1)
        out_ref[half:, lanes] = jnp.concatenate([first[:, HD:], second[:, HD:]], axis=1)

    def place_pairs(odd):
        for pair in range(H // 2):
            first, second = pieces[2 * pair + odd][...], pieces[2 * pair + 1 - odd][...]
            target = (me // 2) ^ pair
            at = pl.multiple_of(width + target * 128, 128)
            out_ref[:, pl.ds(at, 128)] = jnp.concatenate([first[:, :HD], second[:, :HD]], axis=1)
            at = pl.multiple_of(2 * width + target * 128, 128)
            out_ref[:, pl.ds(at, 128)] = jnp.concatenate([first[:, HD:], second[:, HD:]], axis=1)

    pl.when(me % 2 == 0)(lambda: place_pairs(0))
    pl.when(me % 2 == 1)(lambda: place_pairs(1))


def finish(me, dq, pieces):
    return call(
        finish_kernel,
        jax.ShapeDtypeStruct((TOK, 3 * H * HD), jnp.bfloat16),
        [SMEM] + [VMEM] * (1 + COLS),
        VMEM,
        nbytes=6 << 20,
    )(me, dq, *pieces)


def swap(x, axis):
    return lax.all_to_all(x, axis, split_axis=0, concat_axis=0, tiled=True)


def ranks(owner):
    chosen = (
        owner.reshape(1, BLOCKS, BLK) == jnp.arange(OWNERS, dtype=jnp.int32)[:, None, None]
    ).astype(jnp.bfloat16)
    upto = jnp.triu(jnp.ones((BLK, BLK), jnp.bfloat16))
    inside = jnp.einsum("obi,ij->obj", chosen, upto, preferred_element_type=jnp.float32)
    totals = inside[:, :, -1]
    before = jnp.einsum(
        "ob,bc->oc",
        totals.astype(jnp.bfloat16),
        jnp.triu(jnp.ones((BLOCKS, BLOCKS), jnp.bfloat16), 1),
        preferred_element_type=jnp.float32,
    )
    rank = jnp.sum(chosen.astype(jnp.float32) * (inside + before[:, :, None]), axis=0) - 1.0
    counts = jnp.sum(totals, axis=1)
    return rank.reshape(-1).astype(jnp.int32), counts.astype(jnp.int32)


def per_device(queries, key_states, value_states, grad_output, block_lists, dest_rows):
    me = jnp.stack([lax.axis_index("own"), lax.axis_index("ctx")]).astype(jnp.int32)
    coded = interleave_with_dest(dest_rows[0].reshape(4, 128), key_states[0], value_states[0])
    coded = swap(coded, "ctx")
    qg = swap(interleave(queries[0], grad_output[0]), "ctx").reshape(LENGTH, 2 * HD)

    codes = coded[:, TOK : TOK + 8, :].astype(jnp.int32)
    coarse, fine = codes[:, :4].reshape(COLS, TOK), codes[:, 4:].reshape(COLS, TOK)
    columns = jnp.arange(COLS, dtype=jnp.int32)[:, None]
    pool_rows = (columns * TOK + (coarse % 4) * 128 + fine).reshape(-1)
    owner = (coarse // 4).reshape(-1)
    rank, counts = ranks(owner)
    rows = place(owner * STRIDE + rank, pool_rows, counts)
    rows = swap(rows.reshape(OWNERS, 1, STRIDE), "own").reshape(OWNERS, STRIDE)
    largest = jnp.max(rows[:, CAP_MAX : CAP_MAX + OWNERS])

    dq, dkv = attention(
        block_lists[0].reshape(-1), qg, coded.reshape(COLS * CODED, 2 * HD)
    )

    def route(cap):
        def branch(me, owner, rank, rows, dq, dkv):
            slots = owner * cap + rank
            dkv_packed = pack(cap, False, slots, dkv)
            dkv_packed, dq = lax.optimization_barrier((dkv_packed, dq))
            dkv_sent = swap(dkv_packed, "own")
            dq_packed = pack(cap, True, slots, dq)
            dkv_sent, dq_packed = lax.optimization_barrier((dkv_sent, dq_packed))
            dq_sent = swap(dq_packed, "own")
            pieces = unpack(cap, False, me, rows, dkv_sent)
            pieces = [pieces[0]] + [
                lax.ppermute(pieces[d], "ctx", [(i, i ^ d) for i in range(COLS)])
                for d in range(1, COLS)
            ]
            *early, dq_sent = lax.optimization_barrier((*pieces[:EARLY], dq_sent))
            pieces = early + pieces[EARLY:]
            dq_home = swap(unpack(cap, True, me, rows, dq_sent), "ctx")
            return finish(me, dq_home, pieces)

        return branch

    which = jnp.sum((largest > jnp.array(CLASSES[:-1], jnp.int32)).astype(jnp.int32))
    out = lax.switch(
        which, [route(cap) for cap in CLASSES], me, owner, rank, rows.reshape(-1), dq, dkv
    )
    return out[None]


def solution(mesh):
    in_specs = (
        P("own", "ctx", None),
        P("own", "ctx", None),
        P("own", "ctx", None),
        P("own", "ctx", None),
        P("ctx", None, None),
        P("own", "ctx"),
    )
    out_specs = P("own", "ctx", None)
    return jax.shard_map(
        per_device, mesh=mesh, in_specs=in_specs, out_specs=out_specs, check_vma=False
    )
```

```python
import functools

import jax
import jax.numpy as jnp
from jax import lax
from jax.experimental import pallas as pl
from jax.experimental.pallas import tpu as pltpu
from jax.sharding import PartitionSpec as P

H = 16
HD = 64
BLK = 128
KB = 8
COLS = 16
TOK = 512
OWNERS = 16
LENGTH = 8192
BLOCKS = LENGTH // BLK
CLASSES = (640, 704, 768, 832, 896, 960, 1024, 1280, 2048)
CAP_MAX = 2048
STRIDE = CAP_MAX + 128
CODED = TOK + 16
VMEM_LIMIT = 60 * 1024 * 1024
LOG2E = 1.4426950408889634

VMEM = pl.BlockSpec(memory_space=pltpu.VMEM)
SMEM = pl.BlockSpec(memory_space=pltpu.SMEM)
PARAMS = pltpu.CompilerParams(vmem_limit_bytes=VMEM_LIMIT)


def call(kernel, out_shape, in_specs, out_specs, scratch=(), flops=0, nbytes=1 << 20):
    return pl.pallas_call(
        kernel,
        out_shape=out_shape,
        in_specs=in_specs,
        out_specs=out_specs,
        scratch_shapes=list(scratch),
        compiler_params=PARAMS,
        cost_estimate=pl.CostEstimate(flops=flops, bytes_accessed=nbytes, transcendentals=0),
    )


def interleave_kernel(a_ref, b_ref, out_ref):
    for pair in range(H // 2):
        lanes = slice(pair * 128, pair * 128 + 128)
        a = a_ref[:, lanes]
        b = b_ref[:, lanes]
        out_ref[2 * pair, :TOK] = jnp.concatenate([a[:, :HD], b[:, :HD]], axis=1)
        out_ref[2 * pair + 1, :TOK] = jnp.concatenate([a[:, HD:], b[:, HD:]], axis=1)


def interleave_with_dest_kernel(dest_ref, a_ref, b_ref, out_ref):
    interleave_kernel(a_ref, b_ref, out_ref)
    dest = dest_ref[...]
    coarse = (dest // LENGTH) * 4 + (dest % TOK) // 128
    codes = jnp.concatenate(
        [coarse, dest % 128, jnp.zeros((8, 128), jnp.int32)], axis=0
    ).astype(jnp.float32).astype(jnp.bfloat16)
    for head in range(H):
        out_ref[head, TOK:] = codes


def interleave(a, b):
    return call(
        interleave_kernel,
        jax.ShapeDtypeStruct((H, TOK, 2 * HD), jnp.bfloat16),
        [VMEM, VMEM],
        VMEM,
        nbytes=1 << 22,
    )(a, b)


def interleave_with_dest(dest, a, b):
    return call(
        interleave_with_dest_kernel,
        jax.ShapeDtypeStruct((H, CODED, 2 * HD), jnp.bfloat16),
        [VMEM, VMEM, VMEM],
        VMEM,
        nbytes=1 << 22,
    )(dest, a, b)


STEP = 4
DOT = (((1,), (0,)), ((), ()))


def dot(a, b):
    return lax.dot_general(a, b, DOT, preferred_element_type=jnp.float32)


def coded_rows(block):
    return pl.ds(pl.multiple_of((block // 4) * CODED + (block % 4) * BLK, 16), BLK)


def plain_rows(block):
    return pl.ds(pl.multiple_of(block * BLK, BLK), BLK)


def weights_kernel(lists_ref, kq_ref, weights_ref, kt_ref):
    for u in range(STEP):
        block = pl.program_id(0) * STEP + u
        turned = kq_ref[coded_rows(block), :].T
        kt_ref[:, u * BLK : (u + 1) * BLK] = turned[:HD]
        queries = jnp.concatenate([turned[HD:], jnp.zeros((HD, BLK), jnp.bfloat16)], axis=0)
        chosen = [lists_ref[block * KB + j] for j in range(KB)]
        scores = [dot(kq_ref[coded_rows(c), :], queries) for c in chosen]
        top = functools.reduce(jnp.maximum, scores)
        row_max = jnp.max(top, axis=0, keepdims=True)
        exps = [jnp.exp2((s - row_max) * (0.125 * LOG2E)) for s in scores]
        total = functools.reduce(jnp.add, exps)
        inverse = 1.0 / jnp.sum(total, axis=0, keepdims=True)
        for j in range(KB):
            weights_ref[u, j * BLK : (j + 1) * BLK, :] = (exps[j] * inverse).astype(jnp.bfloat16)


def grid_call(kernel, out_shape, in_specs, out_specs, nbytes, flops):
    return pl.pallas_call(
        kernel,
        out_shape=out_shape,
        grid_spec=pltpu.PrefetchScalarGridSpec(
            num_scalar_prefetch=1,
            grid=(BLOCKS // STEP,),
            in_specs=in_specs,
            out_specs=out_specs,
        ),
        compiler_params=pltpu.CompilerParams(
            vmem_limit_bytes=VMEM_LIMIT, dimension_semantics=("arbitrary",)
        ),
        cost_estimate=pl.CostEstimate(flops=flops, bytes_accessed=nbytes, transcendentals=0),
    )


def whole(rows):
    return pl.BlockSpec((rows, 2 * HD), lambda i, lists: (0, 0))


WEIGHTS = pl.BlockSpec((STEP, KB * BLK, BLK), lambda i, lists: (i, 0, 0))


def softmax_weights(lists, kq):
    return grid_call(
        weights_kernel,
        (
            jax.ShapeDtypeStruct((BLOCKS, KB * BLK, BLK), jnp.bfloat16),
            jax.ShapeDtypeStruct((HD, LENGTH), jnp.bfloat16),
        ),
        [whole(COLS * CODED)],
        (WEIGHTS, pl.BlockSpec((HD, STEP * BLK), lambda i, lists: (0, i))),
        20 << 20,
        20 << 30,
    )(lists, kq)


def value_kernel(lists_ref, weights_ref, vg_ref, dv_ref):
    @pl.when(pl.program_id(0) == 0)
    def _():
        dv_ref[...] = jnp.zeros_like(dv_ref)

    for u in range(STEP):
        block = pl.program_id(0) * STEP + u
        vg = vg_ref[plain_rows(block), :]
        grads = jnp.concatenate([vg[:, HD:], jnp.zeros((BLK, HD), jnp.bfloat16)], axis=1)
        for j in range(KB):
            part = dot(weights_ref[u, j * BLK : (j + 1) * BLK, :], grads)
            at = plain_rows(lists_ref[block * KB + j])
            dv_ref[at, :] = dv_ref[at, :] + part


def value_grads(lists, weights, vg):
    return grid_call(
        value_kernel,
        jax.ShapeDtypeStruct((LENGTH, 2 * HD), jnp.float32),
        [WEIGHTS, whole(LENGTH)],
        whole(LENGTH),
        20 << 20,
        10 << 30,
    )(lists, weights, vg)


def query_key_kernel(lists_ref, weights_ref, kq_ref, vg_ref, kt_ref, out_ref):
    lane = lax.broadcasted_iota(jnp.int32, (BLK, 2 * HD), 1)

    @pl.when(pl.program_id(0) == 0)
    def _():
        out_ref[...] = jnp.zeros_like(out_ref)

    for u in range(STEP):
        block = pl.program_id(0) * STEP + u
        turned = vg_ref[plain_rows(block), :].T
        grads = jnp.concatenate([turned[HD:], jnp.zeros((HD, BLK), jnp.bfloat16)], axis=0)
        kq = kq_ref[coded_rows(block), :]
        queries = jnp.where(lane >= HD, kq, jnp.zeros_like(kq))
        chosen = [lists_ref[block * KB + j] for j in range(KB)]
        slopes = [dot(vg_ref[plain_rows(c), :], grads) for c in chosen]
        weights = [
            weights_ref[u, j * BLK : (j + 1) * BLK, :].astype(jnp.float32) for j in range(KB)
        ]
        mixed = functools.reduce(jnp.add, [w * s for w, s in zip(weights, slopes)])
        delta = jnp.sum(mixed, axis=0, keepdims=True)
        dq = jnp.zeros((HD, BLK), jnp.float32)
        for j in range(0, KB, 2):
            pair = [
                (weights[i] * (slopes[i] - delta)).astype(jnp.bfloat16) for i in (j, j + 1)
            ]
            for i in (j, j + 1):
                at = plain_rows(chosen[i])
                out_ref[at, :] = out_ref[at, :] + dot(pair[i - j], queries)
            keys = [kt_ref[:, plain_rows(chosen[i])] for i in (j, j + 1)]
            dq = dq + dot(jnp.concatenate(keys, axis=1), jnp.concatenate(pair, axis=0))
        dq = jnp.concatenate([dq, jnp.zeros((HD, BLK), jnp.float32)], axis=0).T
        out_ref[plain_rows(block), :] = out_ref[plain_rows(block), :] + dq

    @pl.when(pl.program_id(0) == BLOCKS // STEP - 1)
    def _():
        out_ref[...] = out_ref[...] * 0.125


def query_key_grads(lists, weights, kq, vg, kt):
    return grid_call(
        query_key_kernel,
        jax.ShapeDtypeStruct((LENGTH, 2 * HD), jnp.float32),
        [
            WEIGHTS,
            whole(COLS * CODED),
            whole(LENGTH),
            pl.BlockSpec((HD, LENGTH), lambda i, lists: (0, 0)),
        ],
        whole(LENGTH),
        24 << 20,
        30 << 30,
    )(lists, weights, kq, vg, kt)


def place_kernel(me_ref, slots_ref, pool_rows_ref, counts_ref, rows_ref):
    for d in range(OWNERS):
        first = d * STRIDE + counts_ref[me_ref[0] ^ d]
        for k in range(8):
            rows_ref[first + k] = LENGTH

    def body(i, carry):
        for k in range(16):
            at = i * 16 + k
            rows_ref[slots_ref[at]] = pool_rows_ref[at]
        return carry

    lax.fori_loop(0, LENGTH // 16, body, 0)
    for d in range(OWNERS):
        for k in range(OWNERS):
            rows_ref[d * STRIDE + CAP_MAX + k] = counts_ref[k]


def place(me, slots, pool_rows, counts):
    return call(
        place_kernel,
        jax.ShapeDtypeStruct((OWNERS * STRIDE,), jnp.int32),
        [SMEM, SMEM, SMEM, SMEM],
        SMEM,
        nbytes=16 << 20,
    )(me, slots, pool_rows, counts)


def pack_kernel(cap, split, slots_ref, table_ref, out_ref, held):
    def body(i, carry):
        for k in range(16):
            at = i * 16 + k
            held[pl.ds(slots_ref[at], 1), :] = table_ref[pl.ds(at, 1), :]
        return carry

    lax.fori_loop(0, LENGTH // 16, body, 0)
    half = cap // 2
    for owner in range(OWNERS):
        if split:
            left = held[owner * cap : owner * cap + half, :HD]
            right = held[owner * cap + half : (owner + 1) * cap, :HD]
            out_ref[owner] = jnp.concatenate([left, right], axis=1).astype(jnp.bfloat16)
        else:
            out_ref[owner] = held[owner * cap : (owner + 1) * cap, :].astype(jnp.bfloat16)


def pack(cap, split, slots, table):
    return call(
        functools.partial(pack_kernel, cap, split),
        jax.ShapeDtypeStruct((OWNERS, cap // 2 if split else cap, 2 * HD), jnp.bfloat16),
        [SMEM, VMEM],
        VMEM,
        [pltpu.VMEM((OWNERS * cap, 2 * HD), jnp.float32)],
        nbytes=16 << 20,
    )(slots, table)


def unpack_kernel(cap, split, me_ref, rows_ref, in_ref, *refs):
    *outs, held, placed = refs
    me_own, me_ctx = me_ref[0], me_ref[1]
    half = cap // 2
    for source in range(OWNERS):
        if split:
            x = in_ref[source].astype(jnp.float32)
            held[source * cap : source * cap + half, :HD] = x[:, :HD]
            held[source * cap + half : (source + 1) * cap, :HD] = x[:, HD:]
        else:
            held[source * cap : (source + 1) * cap, :] = in_ref[source].astype(jnp.float32)
    for source in range(OWNERS):
        listed = (me_own ^ source) * STRIDE
        count = rows_ref[listed + CAP_MAX + me_own]

        def body(i, carry, source=source, listed=listed):
            first = listed + i * 8
            for k in range(8):
                placed[pl.ds(rows_ref[first + k], 1), :] = held[
                    pl.ds(source * cap + i * 8 + k, 1), :
                ]
            return carry

        lax.fori_loop(0, (count + 7) // 8, body, 0)
    if split:
        for d in range(COLS):
            first = pl.multiple_of((me_ctx ^ d) * TOK, TOK)
            left = placed[pl.ds(first, TOK // 2), :HD]
            right = placed[pl.ds(first + TOK // 2, TOK // 2), :HD]
            outs[d][...] = jnp.concatenate([left, right], axis=1).astype(jnp.bfloat16)
    else:
        (out_ref,) = outs
        for column in range(COLS):
            out_ref[column] = placed[column * TOK : (column + 1) * TOK, :].astype(jnp.bfloat16)


def unpack(cap, split, me, rows, buckets):
    piece = jax.ShapeDtypeStruct((TOK // 2, 2 * HD), jnp.bfloat16)
    every = jax.ShapeDtypeStruct((COLS, TOK, 2 * HD), jnp.bfloat16)
    return call(
        functools.partial(unpack_kernel, cap, split),
        [piece] * COLS if split else every,
        [SMEM, SMEM, VMEM],
        [VMEM] * COLS if split else VMEM,
        [
            pltpu.VMEM((OWNERS * cap, 2 * HD), jnp.float32),
            pltpu.VMEM((LENGTH + 8, 2 * HD), jnp.float32),
        ],
        nbytes=16 << 20,
    )(me, rows, buckets)


def finish_kernel(me_ref, dqk_ref, *refs):
    *pieces, out_ref = refs
    me = me_ref[1]
    half = TOK // 2
    width = H * HD
    for pair in range(H // 2):
        first, second = dqk_ref[2 * pair], dqk_ref[2 * pair + 1]
        at = pair * 128
        out_ref[:, at : at + 128] = jnp.concatenate([first[:, :HD], second[:, :HD]], axis=1)
        at = width + pair * 128
        out_ref[:, at : at + 128] = jnp.concatenate([first[:, HD:], second[:, HD:]], axis=1)

    def place_pairs(odd):
        for pair in range(H // 2):
            first, second = pieces[2 * pair + odd][...], pieces[2 * pair + 1 - odd][...]
            lanes = pl.ds(pl.multiple_of(2 * width + ((me // 2) ^ pair) * 128, 128), 128)
            out_ref[:half, lanes] = jnp.concatenate([first[:, :HD], second[:, :HD]], axis=1)
            out_ref[half:, lanes] = jnp.concatenate([first[:, HD:], second[:, HD:]], axis=1)

    pl.when(me % 2 == 0)(lambda: place_pairs(0))
    pl.when(me % 2 == 1)(lambda: place_pairs(1))


def finish(me, dqk, pieces):
    return call(
        finish_kernel,
        jax.ShapeDtypeStruct((TOK, 3 * H * HD), jnp.bfloat16),
        [SMEM] + [VMEM] * (1 + COLS),
        VMEM,
        nbytes=6 << 20,
    )(me, dqk, *pieces)


def swap(x, axis):
    return lax.all_to_all(x, axis, split_axis=0, concat_axis=0, tiled=True)


def ranks(owner):
    chosen = (
        owner.reshape(1, BLOCKS, BLK) == jnp.arange(OWNERS, dtype=jnp.int32)[:, None, None]
    ).astype(jnp.bfloat16)
    upto = jnp.triu(jnp.ones((BLK, BLK), jnp.bfloat16))
    inside = jnp.einsum("obi,ij->obj", chosen, upto, preferred_element_type=jnp.float32)
    totals = inside[:, :, -1]
    before = jnp.einsum(
        "ob,bc->oc",
        totals.astype(jnp.bfloat16),
        jnp.triu(jnp.ones((BLOCKS, BLOCKS), jnp.bfloat16), 1),
        preferred_element_type=jnp.float32,
    )
    rank = jnp.sum(chosen.astype(jnp.float32) * (inside + before[:, :, None]), axis=0) - 1.0
    counts = jnp.sum(totals, axis=1)
    return rank.reshape(-1).astype(jnp.int32), counts.astype(jnp.int32)


def exchange(pieces, axis):
    return [pieces[0]] + [
        lax.ppermute(pieces[d], axis, [(i, i ^ d) for i in range(16)]) for d in range(1, 16)
    ]


def per_device(queries, key_states, value_states, grad_output, block_lists, dest_rows):
    me = jnp.stack([lax.axis_index("own"), lax.axis_index("ctx")]).astype(jnp.int32)
    lists = block_lists[0].reshape(-1)
    coded = interleave_with_dest(dest_rows[0].reshape(4, 128), key_states[0], queries[0])
    coded = swap(coded, "ctx")
    kq = coded.reshape(COLS * CODED, 2 * HD)
    weights, kt = softmax_weights(lists, kq)
    vg = swap(interleave(value_states[0], grad_output[0]), "ctx").reshape(LENGTH, 2 * HD)

    codes = coded[:, TOK : TOK + 8, :].astype(jnp.int32)
    coarse, fine = codes[:, :4].reshape(COLS, TOK), codes[:, 4:].reshape(COLS, TOK)
    columns = jnp.arange(COLS, dtype=jnp.int32)[:, None]
    pool_rows = (columns * TOK + (coarse % 4) * 128 + fine).reshape(-1)
    owner = (coarse // 4).reshape(-1)
    rank, counts = ranks(owner)
    most = jnp.full((OWNERS, 1, 128), jnp.max(counts), jnp.int32)
    weights, most, vg = lax.optimization_barrier((weights, most, vg))
    largest = jnp.max(swap(most, "own"))

    dv = value_grads(lists, weights, vg)

    def route(cap):
        def branch(me, lists, owner, rank, pool_rows, counts, weights, kq, kt, vg, dv):
            slots = owner * cap + rank
            dv_packed = pack(cap, True, slots, dv)
            dv_packed, weights = lax.optimization_barrier((dv_packed, weights))
            dv_sent = swap(dv_packed, "own")
            dqk_packed = pack(cap, False, slots, query_key_grads(lists, weights, kq, vg, kt))
            dv_sent, dqk_packed, pool_rows = lax.optimization_barrier(
                (dv_sent, dqk_packed, pool_rows)
            )
            dqk_sent = swap(dqk_packed, "own")
            rows = place(me, (owner ^ me[0]) * STRIDE + rank, pool_rows, counts)
            rows = exchange([rows[d * STRIDE : (d + 1) * STRIDE] for d in range(OWNERS)], "own")
            rows = jnp.concatenate(rows)
            pieces = exchange(unpack(cap, True, me, rows, dv_sent), "ctx")
            *pieces, dqk_sent = lax.optimization_barrier((*pieces, dqk_sent))
            return swap(unpack(cap, False, me, rows, dqk_sent), "ctx"), *pieces

        return branch

    which = jnp.sum((largest > jnp.array(CLASSES[:-1], jnp.int32)).astype(jnp.int32))
    dqk, *pieces = lax.switch(
        which,
        [route(cap) for cap in CLASSES],
        *(me, lists, owner, rank, pool_rows, counts, weights, kq, kt, vg, dv),
    )
    return finish(me, dqk, pieces)[None]


def solution(mesh):
    in_specs = (
        P("own", "ctx", None),
        P("own", "ctx", None),
        P("own", "ctx", None),
        P("own", "ctx", None),
        P("ctx", None, None),
        P("own", "ctx"),
    )
    out_specs = P("own", "ctx", None)
    return jax.shard_map(
        per_device, mesh=mesh, in_specs=in_specs, out_specs=out_specs, check_vma=False
    )
```

```python
import functools

import jax
import jax.numpy as jnp
from jax import lax
from jax.experimental import pallas as pl
from jax.experimental.pallas import tpu as pltpu
from jax.sharding import PartitionSpec as P

H = 16
HD = 64
BLK = 128
KB = 8
COLS = 16
TOK = 512
OWNERS = 16
LENGTH = 8192
BLOCKS = LENGTH // BLK
CLASSES = (704, 768, 832, 896, 960, 1024, 1152, 2048)
CAP_MAX = 2048
STRIDE = CAP_MAX + 128
CODED = TOK + 16
VMEM_LIMIT = 60 * 1024 * 1024
LOG2E = 1.4426950408889634

VMEM = pl.BlockSpec(memory_space=pltpu.VMEM)
SMEM = pl.BlockSpec(memory_space=pltpu.SMEM)
PARAMS = pltpu.CompilerParams(vmem_limit_bytes=VMEM_LIMIT)


def call(kernel, out_shape, in_specs, out_specs, scratch=(), flops=0, nbytes=1 << 20):
    return pl.pallas_call(
        kernel,
        out_shape=out_shape,
        in_specs=in_specs,
        out_specs=out_specs,
        scratch_shapes=list(scratch),
        compiler_params=PARAMS,
        cost_estimate=pl.CostEstimate(flops=flops, bytes_accessed=nbytes, transcendentals=0),
    )


def interleave_kernel(a_ref, b_ref, out_ref):
    for pair in range(H // 2):
        lanes = slice(pair * 128, pair * 128 + 128)
        a = a_ref[:, lanes]
        b = b_ref[:, lanes]
        out_ref[2 * pair, :TOK] = jnp.concatenate([a[:, :HD], b[:, :HD]], axis=1)
        out_ref[2 * pair + 1, :TOK] = jnp.concatenate([a[:, HD:], b[:, HD:]], axis=1)


def interleave_with_dest_kernel(dest_ref, a_ref, b_ref, out_ref):
    interleave_kernel(a_ref, b_ref, out_ref)
    dest = dest_ref[...]
    coarse = (dest // LENGTH) * 4 + (dest % TOK) // 128
    codes = jnp.concatenate(
        [coarse, dest % 128, jnp.zeros((8, 128), jnp.int32)], axis=0
    ).astype(jnp.float32).astype(jnp.bfloat16)
    for head in range(H):
        out_ref[head, TOK:] = codes


def interleave(a, b):
    return call(
        interleave_kernel,
        jax.ShapeDtypeStruct((H, TOK, 2 * HD), jnp.bfloat16),
        [VMEM, VMEM],
        VMEM,
        nbytes=1 << 22,
    )(a, b)


def interleave_with_dest(dest, a, b):
    return call(
        interleave_with_dest_kernel,
        jax.ShapeDtypeStruct((H, CODED, 2 * HD), jnp.bfloat16),
        [VMEM, VMEM, VMEM],
        VMEM,
        nbytes=1 << 22,
    )(dest, a, b)


STEP = 4
DOT = (((1,), (0,)), ((), ()))


def dot(a, b):
    return lax.dot_general(a, b, DOT, preferred_element_type=jnp.float32)


def coded_rows(block):
    return pl.ds(pl.multiple_of((block // 4) * CODED + (block % 4) * BLK, 16), BLK)


def plain_rows(block):
    return pl.ds(pl.multiple_of(block * BLK, BLK), BLK)


def weights_kernel(lists_ref, kq_ref, weights_ref, kt_ref):
    for u in range(STEP):
        block = pl.program_id(0) * STEP + u
        turned = kq_ref[coded_rows(block), :].T
        kt_ref[:, u * BLK : (u + 1) * BLK] = turned[:HD]
        queries = jnp.concatenate([turned[HD:], jnp.zeros((HD, BLK), jnp.bfloat16)], axis=0)
        chosen = [lists_ref[block * KB + j] for j in range(KB)]
        scores = [dot(kq_ref[coded_rows(c), :], queries) for c in chosen]
        top = functools.reduce(jnp.maximum, scores)
        row_max = jnp.max(top, axis=0, keepdims=True)
        exps = [jnp.exp2((s - row_max) * (0.125 * LOG2E)) for s in scores]
        total = functools.reduce(jnp.add, exps)
        inverse = 1.0 / jnp.sum(total, axis=0, keepdims=True)
        for j in range(KB):
            weights_ref[u, j * BLK : (j + 1) * BLK, :] = (exps[j] * inverse).astype(jnp.bfloat16)


def grid_call(kernel, out_shape, in_specs, out_specs, nbytes, flops):
    return pl.pallas_call(
        kernel,
        out_shape=out_shape,
        grid_spec=pltpu.PrefetchScalarGridSpec(
            num_scalar_prefetch=1,
            grid=(BLOCKS // STEP,),
            in_specs=in_specs,
            out_specs=out_specs,
        ),
        compiler_params=pltpu.CompilerParams(
            vmem_limit_bytes=VMEM_LIMIT, dimension_semantics=("arbitrary",)
        ),
        cost_estimate=pl.CostEstimate(flops=flops, bytes_accessed=nbytes, transcendentals=0),
    )


def whole(rows):
    return pl.BlockSpec((rows, 2 * HD), lambda i, lists: (0, 0))


WEIGHTS = pl.BlockSpec((STEP, KB * BLK, BLK), lambda i, lists: (i, 0, 0))


def softmax_weights(lists, kq):
    return grid_call(
        weights_kernel,
        (
            jax.ShapeDtypeStruct((BLOCKS, KB * BLK, BLK), jnp.bfloat16),
            jax.ShapeDtypeStruct((HD, LENGTH), jnp.bfloat16),
        ),
        [whole(COLS * CODED)],
        (WEIGHTS, pl.BlockSpec((HD, STEP * BLK), lambda i, lists: (0, i))),
        20 << 20,
        20 << 30,
    )(lists, kq)


def value_kernel(lists_ref, weights_ref, vg_ref, dv_ref):
    @pl.when(pl.program_id(0) == 0)
    def _():
        dv_ref[...] = jnp.zeros_like(dv_ref)

    for u in range(STEP):
        block = pl.program_id(0) * STEP + u
        vg = vg_ref[plain_rows(block), :]
        grads = jnp.concatenate([vg[:, HD:], jnp.zeros((BLK, HD), jnp.bfloat16)], axis=1)
        for j in range(KB):
            part = dot(weights_ref[u, j * BLK : (j + 1) * BLK, :], grads)
            at = plain_rows(lists_ref[block * KB + j])
            dv_ref[at, :] = dv_ref[at, :] + part


def value_grads(lists, weights, vg):
    return grid_call(
        value_kernel,
        jax.ShapeDtypeStruct((LENGTH, 2 * HD), jnp.float32),
        [WEIGHTS, whole(LENGTH)],
        whole(LENGTH),
        20 << 20,
        10 << 30,
    )(lists, weights, vg)


def query_key_kernel(lists_ref, weights_ref, kq_ref, vg_ref, kt_ref, out_ref):
    lane = lax.broadcasted_iota(jnp.int32, (BLK, 2 * HD), 1)

    @pl.when(pl.program_id(0) == 0)
    def _():
        out_ref[...] = jnp.zeros_like(out_ref)

    for u in range(STEP):
        block = pl.program_id(0) * STEP + u
        turned = vg_ref[plain_rows(block), :].T
        grads = jnp.concatenate([turned[HD:], jnp.zeros((HD, BLK), jnp.bfloat16)], axis=0)
        kq = kq_ref[coded_rows(block), :]
        queries = jnp.where(lane >= HD, kq, jnp.zeros_like(kq))
        chosen = [lists_ref[block * KB + j] for j in range(KB)]
        slopes = [dot(vg_ref[plain_rows(c), :], grads) for c in chosen]
        weights = [
            weights_ref[u, j * BLK : (j + 1) * BLK, :].astype(jnp.float32) for j in range(KB)
        ]
        mixed = functools.reduce(jnp.add, [w * s for w, s in zip(weights, slopes)])
        delta = jnp.sum(mixed, axis=0, keepdims=True)
        dq = jnp.zeros((HD, BLK), jnp.float32)
        for j in range(0, KB, 2):
            pair = [
                (weights[i] * (slopes[i] - delta)).astype(jnp.bfloat16) for i in (j, j + 1)
            ]
            for i in (j, j + 1):
                at = plain_rows(chosen[i])
                out_ref[at, :] = out_ref[at, :] + dot(pair[i - j], queries)
            keys = [kt_ref[:, plain_rows(chosen[i])] for i in (j, j + 1)]
            dq = dq + dot(jnp.concatenate(keys, axis=1), jnp.concatenate(pair, axis=0))
        dq = jnp.concatenate([dq, jnp.zeros((HD, BLK), jnp.float32)], axis=0).T
        out_ref[plain_rows(block), :] = out_ref[plain_rows(block), :] + dq

    @pl.when(pl.program_id(0) == BLOCKS // STEP - 1)
    def _():
        out_ref[...] = out_ref[...] * 0.125


def query_key_grads(lists, weights, kq, vg, kt):
    return grid_call(
        query_key_kernel,
        jax.ShapeDtypeStruct((LENGTH, 2 * HD), jnp.float32),
        [
            WEIGHTS,
            whole(COLS * CODED),
            whole(LENGTH),
            pl.BlockSpec((HD, LENGTH), lambda i, lists: (0, 0)),
        ],
        whole(LENGTH),
        24 << 20,
        30 << 30,
    )(lists, weights, kq, vg, kt)


def place_kernel(slots_ref, pool_rows_ref, counts_ref, rows_ref):
    for owner in range(OWNERS):
        first = owner * STRIDE + counts_ref[owner]
        for k in range(8):
            rows_ref[first + k] = LENGTH

    def body(i, carry):
        for k in range(16):
            at = i * 16 + k
            rows_ref[slots_ref[at]] = pool_rows_ref[at]
        return carry

    lax.fori_loop(0, LENGTH // 16, body, 0)
    for owner in range(OWNERS):
        for k in range(OWNERS):
            rows_ref[owner * STRIDE + CAP_MAX + k] = counts_ref[k]


def place(slots, pool_rows, counts):
    return call(
        place_kernel,
        jax.ShapeDtypeStruct((OWNERS * STRIDE,), jnp.int32),
        [SMEM, SMEM, SMEM],
        SMEM,
        nbytes=16 << 20,
    )(slots, pool_rows, counts)


def pack_kernel(cap, split, slots_ref, table_ref, out_ref, held):
    def body(i, carry):
        for k in range(16):
            at = i * 16 + k
            held[pl.ds(slots_ref[at], 1), :] = table_ref[pl.ds(at, 1), :]
        return carry

    lax.fori_loop(0, LENGTH // 16, body, 0)
    half = cap // 2
    for owner in range(OWNERS):
        if split:
            left = held[owner * cap : owner * cap + half, :HD]
            right = held[owner * cap + half : (owner + 1) * cap, :HD]
            out_ref[owner] = jnp.concatenate([left, right], axis=1).astype(jnp.bfloat16)
        else:
            out_ref[owner] = held[owner * cap : (owner + 1) * cap, :].astype(jnp.bfloat16)


def pack(cap, split, slots, table):
    return call(
        functools.partial(pack_kernel, cap, split),
        jax.ShapeDtypeStruct((OWNERS, cap // 2 if split else cap, 2 * HD), jnp.bfloat16),
        [SMEM, VMEM],
        VMEM,
        [pltpu.VMEM((OWNERS * cap, 2 * HD), jnp.float32)],
        nbytes=16 << 20,
    )(slots, table)


def unpack_kernel(cap, split, me_ref, rows_ref, in_ref, *refs):
    *outs, held, placed = refs
    me_own, me_ctx = me_ref[0], me_ref[1]
    half = cap // 2
    for source in range(OWNERS):
        if split:
            x = in_ref[source].astype(jnp.float32)
            held[source * cap : source * cap + half, :HD] = x[:, :HD]
            held[source * cap + half : (source + 1) * cap, :HD] = x[:, HD:]
        else:
            held[source * cap : (source + 1) * cap, :] = in_ref[source].astype(jnp.float32)
    for source in range(OWNERS):
        listed = source * STRIDE
        count = rows_ref[listed + CAP_MAX + me_own]

        def body(i, carry, source=source, listed=listed):
            first = listed + i * 8
            for k in range(8):
                placed[pl.ds(rows_ref[first + k], 1), :] = held[
                    pl.ds(source * cap + i * 8 + k, 1), :
                ]
            return carry

        lax.fori_loop(0, (count + 7) // 8, body, 0)
    if split:
        for d in range(COLS):
            first = pl.multiple_of((me_ctx ^ d) * TOK, TOK)
            left = placed[pl.ds(first, TOK // 2), :HD]
            right = placed[pl.ds(first + TOK // 2, TOK // 2), :HD]
            outs[d][...] = jnp.concatenate([left, right], axis=1).astype(jnp.bfloat16)
    else:
        (out_ref,) = outs
        for column in range(COLS):
            out_ref[column] = placed[column * TOK : (column + 1) * TOK, :].astype(jnp.bfloat16)


def unpack(cap, split, me, rows, buckets):
    piece = jax.ShapeDtypeStruct((TOK // 2, 2 * HD), jnp.bfloat16)
    every = jax.ShapeDtypeStruct((COLS, TOK, 2 * HD), jnp.bfloat16)
    return call(
        functools.partial(unpack_kernel, cap, split),
        [piece] * COLS if split else every,
        [SMEM, SMEM, VMEM],
        [VMEM] * COLS if split else VMEM,
        [
            pltpu.VMEM((OWNERS * cap, 2 * HD), jnp.float32),
            pltpu.VMEM((LENGTH + 8, 2 * HD), jnp.float32),
        ],
        nbytes=16 << 20,
    )(me, rows, buckets)


def finish_kernel(me_ref, dqk_ref, dv_ref, out_ref):
    me = me_ref[1]
    half = TOK // 2
    width = H * HD
    for pair in range(H // 2):
        first, second = dqk_ref[2 * pair], dqk_ref[2 * pair + 1]
        at = pair * 128
        out_ref[:, at : at + 128] = jnp.concatenate([first[:, :HD], second[:, :HD]], axis=1)
        at = width + pair * 128
        out_ref[:, at : at + 128] = jnp.concatenate([first[:, HD:], second[:, HD:]], axis=1)

    def place_pairs(odd):
        for pair in range(H // 2):
            first, second = dv_ref[2 * pair + odd], dv_ref[2 * pair + 1 - odd]
            lanes = pl.ds(pl.multiple_of(2 * width + ((me // 2) ^ pair) * 128, 128), 128)
            out_ref[:half, lanes] = jnp.concatenate([first[:, :HD], second[:, :HD]], axis=1)
            out_ref[half:, lanes] = jnp.concatenate([first[:, HD:], second[:, HD:]], axis=1)

    pl.when(me % 2 == 0)(lambda: place_pairs(0))
    pl.when(me % 2 == 1)(lambda: place_pairs(1))


def finish(me, dqk, dv):
    return call(
        finish_kernel,
        jax.ShapeDtypeStruct((TOK, 3 * H * HD), jnp.bfloat16),
        [SMEM, VMEM, VMEM],
        VMEM,
        nbytes=6 << 20,
    )(me, dqk, dv)


def swap(x, axis):
    return lax.all_to_all(x, axis, split_axis=0, concat_axis=0, tiled=True)


def ranks(owner):
    chosen = (
        owner.reshape(1, BLOCKS, BLK) == jnp.arange(OWNERS, dtype=jnp.int32)[:, None, None]
    ).astype(jnp.bfloat16)
    upto = jnp.triu(jnp.ones((BLK, BLK), jnp.bfloat16))
    inside = jnp.einsum("obi,ij->obj", chosen, upto, preferred_element_type=jnp.float32)
    totals = inside[:, :, -1]
    before = jnp.einsum(
        "ob,bc->oc",
        totals.astype(jnp.bfloat16),
        jnp.triu(jnp.ones((BLOCKS, BLOCKS), jnp.bfloat16), 1),
        preferred_element_type=jnp.float32,
    )
    rank = jnp.sum(chosen.astype(jnp.float32) * (inside + before[:, :, None]), axis=0) - 1.0
    counts = jnp.sum(totals, axis=1)
    return rank.reshape(-1).astype(jnp.int32), counts.astype(jnp.int32)


def exchange(pieces, axis):
    return [pieces[0]] + [
        lax.ppermute(pieces[d], axis, [(i, i ^ d) for i in range(16)]) for d in range(1, 16)
    ]


def per_device(queries, key_states, value_states, grad_output, block_lists, dest_rows):
    me = jnp.stack([lax.axis_index("own"), lax.axis_index("ctx")]).astype(jnp.int32)
    lists = block_lists[0].reshape(-1)
    coded = interleave_with_dest(dest_rows[0].reshape(4, 128), key_states[0], queries[0])
    coded = swap(coded, "ctx")
    kq = coded.reshape(COLS * CODED, 2 * HD)
    weights, kt = softmax_weights(lists, kq)
    vg = swap(interleave(value_states[0], grad_output[0]), "ctx").reshape(LENGTH, 2 * HD)

    codes = coded[:, TOK : TOK + 8, :].astype(jnp.int32)
    coarse, fine = codes[:, :4].reshape(COLS, TOK), codes[:, 4:].reshape(COLS, TOK)
    columns = jnp.arange(COLS, dtype=jnp.int32)[:, None]
    pool_rows = (columns * TOK + (coarse % 4) * 128 + fine).reshape(-1)
    owner = (coarse // 4).reshape(-1)
    rank, counts = ranks(owner)
    rows = place(owner * STRIDE + rank, pool_rows, counts)
    weights, rows, vg = lax.optimization_barrier((weights, rows, vg))
    rows = swap(rows.reshape(OWNERS, 1, STRIDE), "own").reshape(OWNERS, STRIDE)
    largest = jnp.max(rows[:, CAP_MAX : CAP_MAX + OWNERS])

    dv = value_grads(lists, weights, vg)

    def route(cap):
        def branch(me, lists, owner, rank, rows, weights, kq, kt, vg, dv):
            slots = owner * cap + rank
            dv_packed = pack(cap, True, slots, dv)
            dv_packed, weights = lax.optimization_barrier((dv_packed, weights))
            dv_sent = swap(dv_packed, "own")
            dqk_packed = pack(cap, False, slots, query_key_grads(lists, weights, kq, vg, kt))
            dv_sent, dqk_packed = lax.optimization_barrier((dv_sent, dqk_packed))
            dqk_sent = swap(dqk_packed, "own")
            dv_home = jnp.stack(exchange(unpack(cap, True, me, rows, dv_sent), "ctx"))
            dv_home, dqk_sent = lax.optimization_barrier((dv_home, dqk_sent))
            return swap(unpack(cap, False, me, rows, dqk_sent), "ctx"), dv_home

        return branch

    which = jnp.sum((largest > jnp.array(CLASSES[:-1], jnp.int32)).astype(jnp.int32))
    dqk, dv = lax.switch(
        which,
        [route(cap) for cap in CLASSES],
        *(me, lists, owner, rank, rows.reshape(-1), weights, kq, kt, vg, dv),
    )
    return finish(me, dqk, dv)[None]


def solution(mesh):
    in_specs = (
        P("own", "ctx", None),
        P("own", "ctx", None),
        P("own", "ctx", None),
        P("own", "ctx", None),
        P("ctx", None, None),
        P("own", "ctx"),
    )
    out_specs = P("own", "ctx", None)
    return jax.shard_map(
        per_device, mesh=mesh, in_specs=in_specs, out_specs=out_specs, check_vma=False
    )
```

```python
import functools

import jax
import jax.numpy as jnp
from jax import lax
from jax.experimental import pallas as pl
from jax.experimental.pallas import tpu as pltpu
from jax.sharding import PartitionSpec as P

H = 16
HD = 64
BLK = 128
KB = 8
COLS = 16
TOK = 512
OWNERS = 16
LENGTH = 8192
BLOCKS = LENGTH // BLK
CLASSES = (704, 768, 832, 896, 960, 1024, 1152, 2048)
ORDER = (2048, 1152, 704, 1024, 960, 896, 768, 832)
CAP_MAX = 2048
STRIDE = CAP_MAX + 128
CODED = TOK + 16
VMEM_LIMIT = 60 * 1024 * 1024
LOG2E = 1.4426950408889634

VMEM = pl.BlockSpec(memory_space=pltpu.VMEM)
SMEM = pl.BlockSpec(memory_space=pltpu.SMEM)
PARAMS = pltpu.CompilerParams(vmem_limit_bytes=VMEM_LIMIT)


def call(kernel, out_shape, in_specs, out_specs, scratch=(), flops=0, nbytes=1 << 20):
    return pl.pallas_call(
        kernel,
        out_shape=out_shape,
        in_specs=in_specs,
        out_specs=out_specs,
        scratch_shapes=list(scratch),
        compiler_params=PARAMS,
        cost_estimate=pl.CostEstimate(flops=flops, bytes_accessed=nbytes, transcendentals=0),
    )


def lane_tile(index):
    return pl.ds(pl.multiple_of(index * 128, 128), 128)


def interleave_kernel(a_ref, b_ref, out_ref):
    def body(pair, carry):
        a = a_ref[:, lane_tile(pair)]
        b = b_ref[:, lane_tile(pair)]
        out_ref[2 * pair, :TOK] = jnp.concatenate([a[:, :HD], b[:, :HD]], axis=1)
        out_ref[2 * pair + 1, :TOK] = jnp.concatenate([a[:, HD:], b[:, HD:]], axis=1)
        return carry

    lax.fori_loop(0, H // 2, body, 0)


def interleave_with_dest_kernel(dest_ref, a_ref, b_ref, out_ref):
    interleave_kernel(a_ref, b_ref, out_ref)
    dest = dest_ref[...]
    coarse = (dest // LENGTH) * 4 + (dest % TOK) // 128
    codes = jnp.concatenate(
        [coarse, dest % 128, jnp.zeros((8, 128), jnp.int32)], axis=0
    ).astype(jnp.float32).astype(jnp.bfloat16)
    for head in range(H):
        out_ref[head, TOK:] = codes


def interleave(a, b):
    return call(
        interleave_kernel,
        jax.ShapeDtypeStruct((H, TOK, 2 * HD), jnp.bfloat16),
        [VMEM, VMEM],
        VMEM,
        nbytes=1 << 22,
    )(a, b)


def interleave_with_dest(dest, a, b):
    return call(
        interleave_with_dest_kernel,
        jax.ShapeDtypeStruct((H, CODED, 2 * HD), jnp.bfloat16),
        [VMEM, VMEM, VMEM],
        VMEM,
        nbytes=1 << 22,
    )(dest, a, b)


STEP = 4
SHORT = 4
DOT = (((1,), (0,)), ((), ()))


def dot(a, b):
    return lax.dot_general(a, b, DOT, preferred_element_type=jnp.float32)


def coded_rows(block):
    return pl.ds(pl.multiple_of((block // 4) * CODED + (block % 4) * BLK, 16), BLK)


def plain_rows(block):
    return pl.ds(pl.multiple_of(block * BLK, BLK), BLK)


def weights_kernel(lists_ref, kq_ref, weights_ref, kt_ref):
    for u in range(STEP):
        block = pl.program_id(0) * STEP + u
        turned = kq_ref[coded_rows(block), :].T
        kt_ref[:, u * BLK : (u + 1) * BLK] = turned[:HD]
        queries = jnp.concatenate([turned[HD:], jnp.zeros((HD, BLK), jnp.bfloat16)], axis=0)
        chosen = [lists_ref[block * KB + j] for j in range(KB)]
        scores = [dot(kq_ref[coded_rows(c), :], queries) for c in chosen]
        top = functools.reduce(jnp.maximum, scores)
        row_max = jnp.max(top, axis=0, keepdims=True)
        exps = [jnp.exp2((s - row_max) * (0.125 * LOG2E)) for s in scores]
        total = functools.reduce(jnp.add, exps)
        inverse = 1.0 / jnp.sum(total, axis=0, keepdims=True)
        for j in range(KB):
            weights_ref[u, j * BLK : (j + 1) * BLK, :] = (exps[j] * inverse).astype(jnp.bfloat16)


def grid_call(kernel, step, out_shape, in_specs, out_specs, nbytes, flops):
    return pl.pallas_call(
        kernel,
        out_shape=out_shape,
        grid_spec=pltpu.PrefetchScalarGridSpec(
            num_scalar_prefetch=1,
            grid=(BLOCKS // step,),
            in_specs=in_specs,
            out_specs=out_specs,
        ),
        compiler_params=pltpu.CompilerParams(
            vmem_limit_bytes=VMEM_LIMIT, dimension_semantics=("arbitrary",)
        ),
        cost_estimate=pl.CostEstimate(flops=flops, bytes_accessed=nbytes, transcendentals=0),
    )


def whole(rows):
    return pl.BlockSpec((rows, 2 * HD), lambda i, lists: (0, 0))


def weights_of(step):
    return pl.BlockSpec((step, KB * BLK, BLK), lambda i, lists: (i, 0, 0))


def softmax_weights(lists, kq):
    return grid_call(
        weights_kernel,
        STEP,
        (
            jax.ShapeDtypeStruct((BLOCKS, KB * BLK, BLK), jnp.bfloat16),
            jax.ShapeDtypeStruct((HD, LENGTH), jnp.bfloat16),
        ),
        [whole(COLS * CODED)],
        (weights_of(STEP), pl.BlockSpec((HD, STEP * BLK), lambda i, lists: (0, i))),
        20 << 20,
        20 << 30,
    )(lists, kq)


def value_kernel(lists_ref, weights_ref, vg_ref, dv_ref):
    @pl.when(pl.program_id(0) == 0)
    def _():
        dv_ref[...] = jnp.zeros_like(dv_ref)

    for u in range(STEP):
        block = pl.program_id(0) * STEP + u
        vg = vg_ref[plain_rows(block), :]
        grads = jnp.concatenate([vg[:, HD:], jnp.zeros((BLK, HD), jnp.bfloat16)], axis=1)
        for j in range(KB):
            part = dot(weights_ref[u, j * BLK : (j + 1) * BLK, :], grads)
            at = plain_rows(lists_ref[block * KB + j])
            dv_ref[at, :] = dv_ref[at, :] + part


def value_grads(lists, weights, vg):
    return grid_call(
        value_kernel,
        STEP,
        jax.ShapeDtypeStruct((LENGTH, 2 * HD), jnp.float32),
        [weights_of(STEP), whole(LENGTH)],
        whole(LENGTH),
        20 << 20,
        10 << 30,
    )(lists, weights, vg)


def query_key_kernel(lists_ref, weights_ref, kq_ref, vg_ref, kt_ref, out_ref):
    lane = lax.broadcasted_iota(jnp.int32, (BLK, 2 * HD), 1)

    @pl.when(pl.program_id(0) == 0)
    def _():
        out_ref[...] = jnp.zeros_like(out_ref)

    for u in range(SHORT):
        block = pl.program_id(0) * SHORT + u
        turned = vg_ref[plain_rows(block), :].T
        grads = jnp.concatenate([turned[HD:], jnp.zeros((HD, BLK), jnp.bfloat16)], axis=0)
        kq = kq_ref[coded_rows(block), :]
        queries = jnp.where(lane >= HD, kq, jnp.zeros_like(kq))
        chosen = [lists_ref[block * KB + j] for j in range(KB)]
        slopes = [dot(vg_ref[plain_rows(c), :], grads) for c in chosen]
        weights = [
            weights_ref[u, j * BLK : (j + 1) * BLK, :].astype(jnp.float32) for j in range(KB)
        ]
        mixed = functools.reduce(jnp.add, [w * s for w, s in zip(weights, slopes)])
        delta = jnp.sum(mixed, axis=0, keepdims=True)
        dq = jnp.zeros((HD, BLK), jnp.float32)
        for j in range(0, KB, 2):
            pair = [
                (weights[i] * (slopes[i] - delta)).astype(jnp.bfloat16) for i in (j, j + 1)
            ]
            for i in (j, j + 1):
                at = plain_rows(chosen[i])
                out_ref[at, :] = out_ref[at, :] + dot(pair[i - j], queries)
            keys = [kt_ref[:, plain_rows(chosen[i])] for i in (j, j + 1)]
            dq = dq + dot(jnp.concatenate(keys, axis=1), jnp.concatenate(pair, axis=0))
        dq = jnp.concatenate([dq, jnp.zeros((HD, BLK), jnp.float32)], axis=0).T
        out_ref[plain_rows(block), :] = out_ref[plain_rows(block), :] + dq

    @pl.when(pl.program_id(0) == BLOCKS // SHORT - 1)
    def _():
        out_ref[...] = out_ref[...] * 0.125


def query_key_grads(lists, weights, kq, vg, kt):
    return grid_call(
        query_key_kernel,
        SHORT,
        jax.ShapeDtypeStruct((LENGTH, 2 * HD), jnp.float32),
        [
            weights_of(SHORT),
            whole(COLS * CODED),
            whole(LENGTH),
            pl.BlockSpec((HD, LENGTH), lambda i, lists: (0, 0)),
        ],
        whole(LENGTH),
        24 << 20,
        30 << 30,
    )(lists, weights, kq, vg, kt)


def place_kernel(both_ref, counts_ref, rows_ref):
    for owner in range(OWNERS):
        first = owner * STRIDE + counts_ref[owner]
        for k in range(8):
            rows_ref[first + k] = LENGTH

    def body(i, carry):
        for k in range(16):
            both = both_ref[i * 16 + k]
            rows_ref[both & 65535] = both >> 16
        return carry

    lax.fori_loop(0, LENGTH // 16, body, 0)
    for owner in range(OWNERS):
        for k in range(OWNERS):
            rows_ref[owner * STRIDE + CAP_MAX + k] = counts_ref[k]


def place(both, counts):
    return call(
        place_kernel,
        jax.ShapeDtypeStruct((OWNERS * STRIDE,), jnp.int32),
        [SMEM, SMEM],
        SMEM,
        nbytes=16 << 20,
    )(both, counts)


def pack_kernel(cap, split, slots_ref, table_ref, out_ref, held):
    def body(i, carry):
        for k in range(16):
            at = i * 16 + k
            held[pl.ds(slots_ref[at], 1), :] = table_ref[pl.ds(at, 1), :]
        return carry

    lax.fori_loop(0, LENGTH // 16, body, 0)
    def emit(owner, carry):
        first = pl.multiple_of(owner * cap, 32)
        if split:
            left = held[pl.ds(first, cap // 2), :HD]
            right = held[pl.ds(pl.multiple_of(first + cap // 2, 16), cap // 2), :HD]
            out_ref[owner] = jnp.concatenate([left, right], axis=1).astype(jnp.bfloat16)
        else:
            out_ref[owner] = held[pl.ds(first, cap), :].astype(jnp.bfloat16)
        return carry

    lax.fori_loop(0, OWNERS, emit, 0)


def pack(cap, split, slots, table):
    return call(
        functools.partial(pack_kernel, cap, split),
        jax.ShapeDtypeStruct((OWNERS, cap // 2 if split else cap, 2 * HD), jnp.bfloat16),
        [SMEM, VMEM],
        VMEM,
        [pltpu.VMEM((OWNERS * cap, 2 * HD), jnp.float32)],
        nbytes=16 << 20,
    )(slots, table)


def unpack_kernel(cap, split, me_ref, rows_ref, in_ref, *refs):
    *outs, held, placed = refs
    me_own, me_ctx = me_ref[0], me_ref[1]
    half = cap // 2

    def widen(source, carry):
        first = pl.multiple_of(source * cap, 32)
        x = in_ref[source].astype(jnp.float32)
        if split:
            held[pl.ds(first, half), :HD] = x[:, :HD]
            held[pl.ds(pl.multiple_of(first + half, 16), half), :HD] = x[:, HD:]
        else:
            held[pl.ds(first, cap), :] = x
        return carry

    lax.fori_loop(0, OWNERS, widen, 0)

    for source in range(OWNERS):
        count = rows_ref[source * STRIDE + CAP_MAX + me_own]

        def body(i, carry, source=source):
            for k in range(8):
                at = i * 8 + k
                placed[pl.ds(rows_ref[source * STRIDE + at], 1), :] = held[
                    pl.ds(source * cap + at, 1), :
                ]
            return carry

        lax.fori_loop(0, (count + 7) // 8, body, 0)
    if split:
        for d in range(COLS):
            first = pl.multiple_of((me_ctx ^ d) * TOK, TOK)
            left = placed[pl.ds(first, TOK // 2), :HD]
            right = placed[pl.ds(first + TOK // 2, TOK // 2), :HD]
            outs[d % 4][d // 4] = jnp.concatenate([left, right], axis=1).astype(jnp.bfloat16)
    else:
        (out_ref,) = outs

        def emit(column, carry):
            rows = pl.ds(pl.multiple_of(column * TOK, TOK), TOK)
            out_ref[column] = placed[rows, :].astype(jnp.bfloat16)
            return carry

        lax.fori_loop(0, COLS, emit, 0)


def unpack(cap, split, me, rows, buckets):
    piece = jax.ShapeDtypeStruct((4, TOK // 2, 2 * HD), jnp.bfloat16)
    every = jax.ShapeDtypeStruct((COLS, TOK, 2 * HD), jnp.bfloat16)
    return call(
        functools.partial(unpack_kernel, cap, split),
        [piece] * 4 if split else every,
        [SMEM, SMEM, VMEM],
        [VMEM] * 4 if split else VMEM,
        [
            pltpu.VMEM((OWNERS * cap, 2 * HD), jnp.float32),
            pltpu.VMEM((LENGTH + 8, 2 * HD), jnp.float32),
        ],
        nbytes=16 << 20,
    )(me, rows, buckets)


def finish_kernel(me_ref, dqk_ref, dv_ref, out_ref):
    me = me_ref[1]
    half = TOK // 2

    def body(pair, carry):
        first, second = dqk_ref[2 * pair], dqk_ref[2 * pair + 1]
        out_ref[:, lane_tile(pair)] = jnp.concatenate([first[:, :HD], second[:, :HD]], axis=1)
        out_ref[:, lane_tile(H // 2 + pair)] = jnp.concatenate(
            [first[:, HD:], second[:, HD:]], axis=1
        )
        odd = me % 2
        first, second = dv_ref[2 * pair + odd], dv_ref[2 * pair + 1 - odd]
        lanes = lane_tile(H + ((me // 2) ^ pair))
        out_ref[:half, lanes] = jnp.concatenate([first[:, :HD], second[:, :HD]], axis=1)
        out_ref[half:, lanes] = jnp.concatenate([first[:, HD:], second[:, HD:]], axis=1)
        return carry

    lax.fori_loop(0, H // 2, body, 0)


def finish(me, dqk, dv):
    return call(
        finish_kernel,
        jax.ShapeDtypeStruct((TOK, 3 * H * HD), jnp.bfloat16),
        [SMEM, VMEM, VMEM],
        VMEM,
        nbytes=6 << 20,
    )(me, dqk, dv)


def swap(x, axis):
    return lax.all_to_all(x, axis, split_axis=0, concat_axis=0, tiled=True)


def ranks(owner):
    chosen = (
        owner.reshape(1, BLOCKS, BLK) == jnp.arange(OWNERS, dtype=jnp.int32)[:, None, None]
    ).astype(jnp.bfloat16)
    upto = jnp.triu(jnp.ones((BLK, BLK), jnp.bfloat16))
    inside = jnp.einsum("obi,ij->obj", chosen, upto, preferred_element_type=jnp.float32)
    totals = inside[:, :, -1]
    before = jnp.einsum(
        "ob,bc->oc",
        totals.astype(jnp.bfloat16),
        jnp.triu(jnp.ones((BLOCKS, BLOCKS), jnp.bfloat16), 1),
        preferred_element_type=jnp.float32,
    )
    rank = jnp.sum(chosen.astype(jnp.float32) * (inside + before[:, :, None]), axis=0) - 1.0
    counts = jnp.sum(totals, axis=1)
    return rank.reshape(-1).astype(jnp.int32), counts.astype(jnp.int32)


def exchange(arrays):
    def hop(arrays, unit):
        return arrays[:1] + [
            lax.ppermute(arrays[j], "ctx", [(k, k ^ (unit * j)) for k in range(COLS)])
            for j in range(1, 4)
        ]

    arrays = hop(list(arrays), 1)
    arrays = hop([jnp.stack([x[i] for x in arrays]) for i in range(4)], 4)
    return jnp.concatenate(arrays)


def per_device(queries, key_states, value_states, grad_output, block_lists, dest_rows):
    me = jnp.stack([lax.axis_index("own"), lax.axis_index("ctx")]).astype(jnp.int32)
    lists = block_lists[0].reshape(-1)
    coded = interleave_with_dest(dest_rows[0].reshape(4, 128), key_states[0], queries[0])
    coded = swap(coded, "ctx")
    kq = coded.reshape(COLS * CODED, 2 * HD)
    weights, kt = softmax_weights(lists, kq)
    vg = swap(interleave(value_states[0], grad_output[0]), "ctx").reshape(LENGTH, 2 * HD)

    codes = coded[:, TOK : TOK + 8, :].astype(jnp.int32)
    coarse, fine = codes[:, :4].reshape(COLS, TOK), codes[:, 4:].reshape(COLS, TOK)
    columns = jnp.arange(COLS, dtype=jnp.int32)[:, None]
    pool_rows = (columns * TOK + (coarse % 4) * 128 + fine).reshape(-1)
    owner = (coarse // 4).reshape(-1)
    rank, counts = ranks(owner)
    rows = place(pool_rows * 65536 + owner * STRIDE + rank, counts)
    weights, rows, vg = lax.optimization_barrier((weights, rows, vg))
    rows = swap(rows.reshape(OWNERS, 1, STRIDE), "own").reshape(OWNERS, STRIDE)
    largest = jnp.max(rows[:, CAP_MAX : CAP_MAX + OWNERS])

    dv = value_grads(lists, weights, vg)

    def route(cap):
        def branch(me, lists, owner, rank, rows, weights, kq, kt, vg, dv):
            slots = owner * cap + rank
            dv_packed = pack(cap, True, slots, dv)
            dv_packed, weights = lax.optimization_barrier((dv_packed, weights))
            dv_sent = swap(dv_packed, "own")
            dqk_packed = pack(cap, False, slots, query_key_grads(lists, weights, kq, vg, kt))
            dv_sent, dqk_packed = lax.optimization_barrier((dv_sent, dqk_packed))
            dqk_sent = swap(dqk_packed, "own")
            dv_home = exchange(unpack(cap, True, me, rows, dv_sent))
            dv_home, dqk_sent = lax.optimization_barrier((dv_home, dqk_sent))
            return swap(unpack(cap, False, me, rows, dqk_sent), "ctx"), dv_home

        return branch

    fit = jnp.sum((largest > jnp.array(CLASSES[:-1], jnp.int32)).astype(jnp.int32))
    places = jnp.array([ORDER.index(cap) for cap in CLASSES], jnp.int32)
    which = jnp.sum(jnp.where(jnp.arange(len(CLASSES)) == fit, places, 0))
    dqk, dv = lax.switch(
        which,
        [route(cap) for cap in ORDER],
        *(me, lists, owner, rank, rows.reshape(-1), weights, kq, kt, vg, dv),
    )
    return finish(me, dqk, dv)[None]


def solution(mesh):
    in_specs = (
        P("own", "ctx", None),
        P("own", "ctx", None),
        P("own", "ctx", None),
        P("own", "ctx", None),
        P("ctx", None, None),
        P("own", "ctx"),
    )
    out_specs = P("own", "ctx", None)
    return jax.shard_map(
        per_device, mesh=mesh, in_specs=in_specs, out_specs=out_specs, check_vma=False
    )
```
